256 devices in a mesh: dp: 32 (over z, y), expert: 8 (over x, core).
Axes of the slice: x: 4, y: 4, z: 8, core: 2. Of those that a mesh axis runs over, the one named last changes fastest.
Arguments:
- grad: bfloat16 [128, 1024, 768], P('expert', 'dp'), may hold values from -1200 to 1200
- momentum: float32 [128, 1024, 768], P('expert', 'dp'), may hold values from -3 to 3
Outputs:
- new_momentum: float32 [128, 1024, 768], P('expert', 'dp')
- update: float32 [128, 1024, 768], P('expert', 'dp')
The draws below stay inside these ranges and needn't reach their ends.
All inputs are finite; a program needn't handle non-finite values.
Results may differ from the reference program's by a relative error of at most 0.0003.
Values sent between devices are 32-bit elements; how exact they have to be, the bound alone decides.
No kernel may reach another device: no remote copies, remote signals or barrier semaphores. Data moves between devices by JAX's collectives and lax.ppermute only.
A program may use at most 64 MiB of HBM per device.

```python
import math
import jax
import jax.numpy as jnp
from jax import lax

R = 1024
C = 768
ITERS = 2
MATS_GRP = 16
MATS = 128


def draw_grad(key, part):
    key = jax.random.fold_in(key, 11)
    first, second, third = jax.random.split(key, 3)
    place = (jnp.arange(MATS, dtype=jnp.float32)[:, None] * R + jnp.arange(R, dtype=jnp.float32)[None, :]) / (MATS * R)
    slice_len = R // (2 * MATS_GRP)
    within = (jnp.arange(R, dtype=jnp.int32) % slice_len).astype(jnp.float32) / slice_len
    inner_rise = jnp.exp(math.log(3.0) * within)[None, :, None]
    row_scale = jnp.exp(jax.random.uniform(second, (MATS, R, 1), jnp.float32, math.log(0.5), math.log(5.0)))
    col_scale = jnp.exp(jax.random.uniform(third, (MATS, 1, C), jnp.float32, math.log(0.5), math.log(5.0)))
    base = jnp.clip(jax.random.normal(first, (MATS, R, C), jnp.float32), -6.0, 6.0)
    rise = jnp.exp(0.5 * math.log(3.0) * place)
    return (base * row_scale * col_scale * inner_rise * rise[:, :, None]).astype(jnp.bfloat16)


def block_levels(own_key, dims, cuts, least, high):
    level, own = 1.0, jax.random.fold_in(own_key, 6)
    for dim, blocks in cuts:
        steps = jnp.exp(jax.random.uniform(jax.random.fold_in(own, dim), (blocks,), jnp.float32, least / len(cuts), high / len(cuts)))
        level = level * jnp.repeat(steps, dims[dim] // blocks).reshape([-1 if axis == dim else 1 for axis in range(len(dims))])
    return level


def normal_values(rng, shape, spread, bound, cuts=(), kind=jnp.bfloat16):
    array = jax.random.normal(rng, shape, jnp.float32) * spread
    if len(cuts) > 0:
        array = block_levels(rng, shape, cuts, -0.22, 0.18) * array
    return jnp.clip(array, min=-bound, max=bound).astype(kind)


def setup_inputs(seed: int = 0) -> dict:
    keys = jax.random.split(jax.random.key(seed), 3)
    return {
        "grad": draw_grad(jax.random.fold_in(keys[2], 71), 0),
        "momentum": normal_values(keys[1], (MATS, R, C), 0.5, 3.0, ((0, 8), (1, 32)), jnp.float32),
    }


def orthogonalize(block):
    block = block / (jnp.sqrt(jnp.sum(block * block)) + 1e-07)
    for step in range(ITERS):
        gram = jnp.dot(block.T, block, precision=lax.Precision.HIGHEST)
        poly = -4.775 * gram + 2.0315 * jnp.dot(gram, gram, precision=lax.Precision.HIGHEST)
        block = 3.4445 * block + jnp.dot(block, poly, precision=lax.Precision.HIGHEST)
    return block

def reference(grad, momentum):
    widened = grad.astype(jnp.float32)
    squares = jnp.sum(widened * widened)
    factor = jnp.minimum(1.0, 0.5 / jnp.sqrt(squares / (MATS * R * C) + 1e-06))
    clipped = widened * factor
    new_momentum = 0.95 * momentum + clipped
    advance = clipped + 0.95 * new_momentum
    finished = lax.map(orthogonalize, advance)
    update = finished * (0.2 * jnp.sqrt(jnp.float32(max(R, C))))
    return (new_momentum, update)
```

```python
import math

import jax
import jax.numpy as jnp
from jax import lax
from jax.sharding import PartitionSpec as P

R = 1024
C = 768
ITERS = 2

A0, A1, A2 = 3.4445, -4.775, 2.0315


def mm(a, b):
    return jnp.dot(a, b, precision=lax.Precision.HIGH, preferred_element_type=jnp.float32)


def gram_of(x):
    return lax.dot_general(
        x, x, (((0,), (0,)), ((), ())),
        precision=lax.Precision.HIGH, preferred_element_type=jnp.float32,
    )


def swap_cores(x):
    n = lax.axis_size("expert")
    return lax.ppermute(x, "expert", [(i, i ^ 1) for i in range(n)])


def global_sum(part):
    n = lax.axis_size("dp") * lax.axis_size("expert")
    tile = jnp.broadcast_to(part, (n, 1, 128))
    got = lax.all_to_all(tile, ("dp", "expert"), split_axis=0, concat_axis=0, tiled=True)
    return jnp.sum(got[:, 0, 0])


def poly(gram):
    eye = jnp.eye(C, dtype=jnp.float32)
    return A0 * eye + (A1 * gram + A2 * mm(gram, gram))


def body(grad, momentum):
    groups, slice_rows, columns = grad.shape
    n_rows = lax.axis_size("dp")
    core = lax.axis_index("expert") % 2
    half = slice_rows // 2
    count = groups * slice_rows * columns * n_rows * lax.axis_size("expert")
    widened = grad.astype(jnp.float32)
    total = global_sum(jnp.sum(widened * widened))
    factor = jnp.minimum(1.0, 0.5 / jnp.sqrt(total / count + 1e-06))
    clipped = widened * factor
    new_momentum = 0.95 * momentum + clipped
    advance = clipped + 0.95 * new_momentum

    keep = lax.dynamic_slice_in_dim(advance, core * half, half, 1)
    give = lax.dynamic_slice_in_dim(advance, (1 - core) * half, half, 1)
    got = swap_cores(give)
    outgoing = jnp.where(
        core == 0, jnp.concatenate([keep, got], 0), jnp.concatenate([got, keep], 0)
    )
    own = lax.all_to_all(outgoing, "dp", split_axis=0, concat_axis=0, tiled=True)
    own = own.reshape(n_rows * half, columns)
    other = swap_cores(own)

    raw = gram_of(own) + gram_of(other)
    norm = jnp.sqrt(jnp.sum(own * own) + jnp.sum(other * other)) + 1e-07
    inverse = 1.0 / norm
    gram = raw * inverse * inverse
    m0 = poly(gram)
    first = mm(own * inverse, m0)
    m1 = poly(mm(mm(gram, m0), m0))
    finished = mm(first, m1) * (0.2 * math.sqrt(max(R, C)))

    back = lax.all_to_all(
        finished.reshape(n_rows, half, columns), "dp", split_axis=0, concat_axis=0, tiled=True
    )
    mine = lax.dynamic_slice_in_dim(back, core * groups, groups, 0)
    theirs = lax.dynamic_slice_in_dim(back, (1 - core) * groups, groups, 0)
    got = swap_cores(theirs)
    update = jnp.where(
        core == 0, jnp.concatenate([mine, got], 1), jnp.concatenate([got, mine], 1)
    )
    return (new_momentum, update)


def solution(mesh):
    in_specs = (P("expert", "dp", None), P("expert", "dp", None))
    out_specs = (P("expert", "dp", None), P("expert", "dp", None))
    return jax.shard_map(body, mesh=mesh, in_specs=in_specs, out_specs=out_specs, check_vma=False)
```

```python
import math

import jax
import jax.numpy as jnp
from jax import lax
from jax.experimental import pallas as pl
from jax.experimental.pallas import tpu as pltpu
from jax.sharding import PartitionSpec as P

R = 1024
C = 768
ITERS = 2
BLOCK = 256
NB = C // BLOCK
PAIRS = [(i, j) for i in range(NB) for j in range(i, NB)]

A0, A1, A2 = 3.4445, -4.775, 2.0315
F32 = jnp.float32
BF16 = jnp.bfloat16

VMEM = pl.BlockSpec(memory_space=pltpu.VMEM)
SMEM = pl.BlockSpec(memory_space=pltpu.SMEM)
HBM = pl.BlockSpec(memory_space=pl.ANY)


def params(mib):
    return pltpu.CompilerParams(vmem_limit_bytes=mib << 20)


def swap_cores(x):
    n = lax.axis_size("expert")
    return lax.ppermute(x, "expert", [(i, i ^ 1) for i in range(n)])


def split(v):
    hi = v.astype(BF16)
    return hi, (v - hi.astype(F32)).astype(BF16)


def dot(a, b):
    return jnp.dot(a, b, preferred_element_type=F32)


def dot3(ah, al, bh, bl):
    return dot(ah, bh) + (dot(ah, bl) + dot(al, bh))


def blk(i):
    return pl.ds(i * BLOCK, BLOCK)


def put_symmetric(h, l, i, j, v):
    h[blk(i), blk(j)], l[blk(i), blk(j)] = split(v)
    if i != j:
        h[blk(j), blk(i)], l[blk(j), blk(i)] = split(v.T)


def split_both_ways(x_ref, xh, xl, th, tl):
    for j in range(NB):
        v = x_ref[:, blk(j)]
        xh[:, blk(j)], xl[:, blk(j)] = split(v)
        th[blk(j), :], tl[blk(j), :] = split(v.T)


def prepare_kernel(core_ref, grad_ref, momentum_ref, sum_ref, give_ref):
    half = grad_ref.shape[1] // 2
    rows = pl.ds(pl.multiple_of((1 - core_ref[0]) * half, half), half)
    total = jnp.zeros(grad_ref.shape[1:], F32)
    for i in range(grad_ref.shape[0]):
        v = grad_ref[i].astype(F32)
        total = total + v * v
        give_ref[0, i] = grad_ref[i, rows, :].astype(F32)
        give_ref[1, i] = momentum_ref[i, rows, :]
    total = jnp.sum(jnp.sum(total, axis=0, keepdims=True), axis=1, keepdims=True)
    sum_ref[...] = jnp.broadcast_to(total[None], sum_ref.shape)


def momentum_kernel(factor_ref, grad_ref, momentum_ref, out_ref):
    factor = factor_ref[:1, :1]
    for i in range(grad_ref.shape[0]):
        out_ref[i] = 0.95 * momentum_ref[i] + grad_ref[i].astype(F32) * factor


def place_kernel(of_core, core_ref, values_ref, *refs):
    out_ref, sem = refs[-2:]
    groups, slice_rows, _ = out_ref.shape
    half = slice_rows // 2
    core = core_ref[0] if of_core else 1 - core_ref[0]
    source = values_ref.at[pl.ds(core * groups, groups)] if of_core else values_ref
    rows = pl.ds(pl.multiple_of(core * half, half), half)
    copy = pltpu.make_async_copy(source, out_ref.at[:, rows, :], sem)
    copy.start()
    copy.wait()


def place(of_core, core, values, shape, before=()):
    return pl.pallas_call(
        lambda *refs: place_kernel(of_core, *refs),
        out_shape=jax.ShapeDtypeStruct(shape, F32),
        in_specs=[SMEM, HBM] + [HBM] * len(before),
        out_specs=HBM,
        scratch_shapes=[pltpu.SemaphoreType.DMA],
        input_output_aliases={2: 0} if before else {},
        compiler_params=params(1),
        name="place",
    )(core, values, *before)


def mix_kernel(count, core_ref, sums_ref, grad_ref, momentum_ref, got_ref, out_ref, factor_ref):
    groups = grad_ref.shape[0]
    half = grad_ref.shape[1] // 2
    core = core_ref[0]
    total = jnp.sum(sums_ref[:, 0, :], axis=0, keepdims=True)[:, :1]
    factor = jnp.minimum(1.0, 0.5 / jnp.sqrt(total / count + 1e-06))
    factor_ref[...] = jnp.broadcast_to(factor, factor_ref.shape)
    rows = pl.ds(pl.multiple_of(core * half, half), half)
    mine = core * groups
    theirs = (1 - core) * groups

    def mix(g, m):
        clipped = g * factor
        return clipped + 0.95 * (0.95 * m + clipped)

    for i in range(groups):
        out_ref[mine + i] = mix(grad_ref[i, rows, :].astype(F32), momentum_ref[i, rows, :])
        out_ref[theirs + i] = mix(got_ref[0, i], got_ref[1, i])


def gram_kernel(x_ref, g_ref, xh, xl, th, tl):
    split_both_ways(x_ref, xh, xl, th, tl)
    for i, j in PAIRS:
        g_ref[blk(i), blk(j)] = dot3(th[blk(i), :], tl[blk(i), :], xh[:, blk(j)], xl[:, blk(j)])


def poly_kernel(xh, xl, part_ref, other_ref, out_ref, raw, yh, yl, th, tl, gh, gl, mh, ml, ph, pl_):
    split_both_ways(other_ref, yh, yl, th, tl)
    shape = (BLOCK, BLOCK)
    eye = (lax.broadcasted_iota(jnp.int32, shape, 0) == lax.broadcasted_iota(jnp.int32, shape, 1)).astype(F32)
    trace = jnp.zeros((1, 1), F32)
    for i, j in PAIRS:
        v = part_ref[blk(i), blk(j)] + dot3(th[blk(i), :], tl[blk(i), :], yh[:, blk(j)], yl[:, blk(j)])
        raw[blk(i), blk(j)] = v
        if i == j:
            trace = trace + jnp.sum(jnp.sum(v * eye, axis=0, keepdims=True), axis=1, keepdims=True)
    inverse = 1.0 / (jnp.sqrt(trace) + 1e-07)
    for i, j in PAIRS:
        v = raw[blk(i), blk(j)] * inverse * inverse
        raw[blk(i), blk(j)] = v
        put_symmetric(gh, gl, i, j, v)

    def polynomial(h, l, oh, ol):
        for i, j in PAIRS:
            v = A1 * raw[blk(i), blk(j)] + A2 * dot3(h[blk(i), :], l[blk(i), :], h[:, blk(j)], l[:, blk(j)])
            if i == j:
                v = v + A0 * eye
            put_symmetric(oh, ol, i, j, v)

    polynomial(gh, gl, mh, ml)
    for i, j in PAIRS:
        put_symmetric(ph, pl_, i, j, dot3(gh[blk(i), :], gl[blk(i), :], mh[:, blk(j)], ml[:, blk(j)]))
    rows = range(out_ref.shape[0] // BLOCK)
    for i in rows:
        for j in range(NB):
            v = dot3(xh[blk(i), :], xl[blk(i), :], mh[:, blk(j)], ml[:, blk(j)]) * inverse
            yh[blk(i), blk(j)], yl[blk(i), blk(j)] = split(v)
    for i, j in PAIRS:
        v = dot3(ph[blk(i), :], pl_[blk(i), :], mh[:, blk(j)], ml[:, blk(j)])
        raw[blk(i), blk(j)] = v
        put_symmetric(gh, gl, i, j, v)
    polynomial(gh, gl, ph, pl_)
    scale = 0.2 * math.sqrt(max(R, C))
    for i in rows:
        for j in range(NB):
            out_ref[blk(i), blk(j)] = scale * dot3(yh[blk(i), :], yl[blk(i), :], ph[:, blk(j)], pl_[:, blk(j)])


def orthogonalize(own, other):
    n = own.shape[0]
    wide, tall, square = ((n, C), (C, n), (C, C))
    part, xh, xl = pl.pallas_call(
        gram_kernel,
        out_shape=(
            jax.ShapeDtypeStruct(square, F32),
            jax.ShapeDtypeStruct(wide, BF16),
            jax.ShapeDtypeStruct(wide, BF16),
        ),
        in_specs=[VMEM],
        out_specs=(VMEM,) * 3,
        scratch_shapes=[pltpu.VMEM(tall, BF16)] * 2,
        compiler_params=params(12),
        name="gram",
    )(own)
    return pl.pallas_call(
        poly_kernel,
        out_shape=jax.ShapeDtypeStruct(wide, F32),
        in_specs=[VMEM] * 4,
        out_specs=VMEM,
        scratch_shapes=[pltpu.VMEM(square, F32)]
        + [pltpu.VMEM(wide, BF16)] * 2
        + [pltpu.VMEM(tall, BF16)] * 2
        + [pltpu.VMEM(square, BF16)] * 6,
        compiler_params=params(24),
        name="poly",
    )(xh, xl, part, other)


def body(grad, momentum):
    groups, slice_rows, columns = grad.shape
    n_rows = lax.axis_size("dp")
    devices = n_rows * lax.axis_size("expert")
    core = lax.axis_index("expert") % 2
    half = slice_rows // 2
    count = groups * slice_rows * columns * devices

    core_index = core.reshape(1)
    tile, give = pl.pallas_call(
        prepare_kernel,
        out_shape=(
            jax.ShapeDtypeStruct((devices, 1, 128), F32),
            jax.ShapeDtypeStruct((2, groups, half, columns), F32),
        ),
        in_specs=[SMEM] + [VMEM] * 2,
        out_specs=(VMEM, VMEM),
        compiler_params=params(8),
        name="prepare",
    )(core_index, grad, momentum)
    sums = lax.all_to_all(tile, ("dp", "expert"), split_axis=0, concat_axis=0, tiled=True)
    got = swap_cores(give)
    outgoing, factor = pl.pallas_call(
        lambda *refs: mix_kernel(count, *refs),
        out_shape=(
            jax.ShapeDtypeStruct((n_rows, half, columns), F32),
            jax.ShapeDtypeStruct((8, 128), F32),
        ),
        in_specs=[SMEM] + [VMEM] * 4,
        out_specs=(VMEM, VMEM),
        compiler_params=params(10),
        name="mix",
    )(core_index, sums, grad, momentum, got)

    own = lax.all_to_all(outgoing, "dp", split_axis=0, concat_axis=0, tiled=True)
    factor, grad, momentum, own = lax.optimization_barrier((factor, grad, momentum, own))
    new_momentum = pl.pallas_call(
        momentum_kernel,
        out_shape=jax.ShapeDtypeStruct(momentum.shape, F32),
        in_specs=[VMEM] * 3,
        out_specs=VMEM,
        compiler_params=params(8),
        name="momentum",
    )(factor, grad, momentum)
    own = own.reshape(n_rows * half, columns)
    finished = orthogonalize(own, swap_cores(own))

    finished, new_momentum = lax.optimization_barrier((finished, new_momentum))
    back = lax.all_to_all(
        finished.reshape(n_rows, half, columns), "dp", split_axis=0, concat_axis=0, tiled=True
    )
    theirs = lax.dynamic_slice_in_dim(back, (1 - core) * groups, groups, 0)
    got = swap_cores(theirs)
    update = place(True, core_index, back, grad.shape)
    update = place(False, core_index, got, grad.shape, (update,))
    return (new_momentum, update)


def solution(mesh):
    in_specs = (P("expert", "dp", None), P("expert", "dp", None))
    out_specs = (P("expert", "dp", None), P("expert", "dp", None))
    return jax.shard_map(body, mesh=mesh, in_specs=in_specs, out_specs=out_specs, check_vma=False)
```

```python
import math

import jax
import jax.numpy as jnp
from jax import lax
from jax.experimental import pallas as pl
from jax.experimental.pallas import tpu as pltpu
from jax.sharding import PartitionSpec as P

R = 1024
C = 768
ITERS = 2
BLOCK = 256
NB = C // BLOCK
PAIRS = [(i, j) for i in range(NB) for j in range(i, NB)]

A0, A1, A2 = 3.4445, -4.775, 2.0315
F32 = jnp.float32
BF16 = jnp.bfloat16

VMEM = pl.BlockSpec(memory_space=pltpu.VMEM)
SMEM = pl.BlockSpec(memory_space=pltpu.SMEM)
HBM = pl.BlockSpec(memory_space=pl.ANY)
PINNED = pl.BlockSpec(memory_space=pltpu.HBM)


def params(mib):
    return pltpu.CompilerParams(vmem_limit_bytes=mib << 20)


def swap_cores(x):
    n = lax.axis_size("expert")
    return lax.ppermute(x, "expert", [(i, i ^ 1) for i in range(n)])


def split(v):
    hi = v.astype(BF16)
    return hi, (v - hi.astype(F32)).astype(BF16)


def dot(a, b):
    return jnp.dot(a, b, preferred_element_type=F32)


def dot3(ah, al, bh, bl):
    return dot(ah, bh) + (dot(ah, bl) + dot(al, bh))


def blk(i):
    return pl.ds(i * BLOCK, BLOCK)


def square(rh, rl, ch, cl, i, j):
    if i != j:
        return dot3(rh[blk(i), :], rl[blk(i), :], ch[:, blk(j)], cl[:, blk(j)])
    cross = dot(rh[blk(i), :], cl[:, blk(j)])
    return dot(rh[blk(i), :], ch[:, blk(j)]) + (cross + cross.T)


def put_symmetric(h, l, i, j, v):
    h[blk(i), blk(j)], l[blk(i), blk(j)] = split(v)
    if i != j:
        h[blk(j), blk(i)], l[blk(j), blk(i)] = split(v.T)


def split_both_ways(x_ref, xh, xl, th, tl):
    for j in range(NB):
        v = x_ref[:, blk(j)]
        xh[:, blk(j)], xl[:, blk(j)] = split(v)
        th[blk(j), :], tl[blk(j), :] = split(v.T)


def halves(core_ref, slice_rows):
    half = slice_rows // 2
    core = core_ref[0]
    return (
        pl.ds(pl.multiple_of(core * half, half), half),
        pl.ds(pl.multiple_of((1 - core) * half, half), half),
    )


def prepare_kernel(core_ref, grad_ref, momentum_ref, sum_ref, keep_ref, give_ref, wide, sems):
    keep, give = halves(core_ref, grad_ref.shape[1])
    copies = [
        pltpu.make_async_copy(grad_ref, wide, sems.at[0]),
        pltpu.make_async_copy(momentum_ref.at[:, give, :], give_ref.at[1], sems.at[1]),
        pltpu.make_async_copy(momentum_ref.at[:, keep, :], keep_ref.at[1], sems.at[2]),
    ]
    for copy in copies:
        copy.start()
    copies[0].wait()
    total = jnp.zeros(give_ref.shape[2:], F32)
    for i in range(wide.shape[0]):
        kept = wide[i, keep, :].astype(F32)
        given = wide[i, give, :].astype(F32)
        total = total + kept * kept + given * given
        keep_ref[0, i] = kept
        give_ref[0, i] = given
    total = jnp.sum(jnp.sum(total, axis=0, keepdims=True), axis=1, keepdims=True)
    sum_ref[...] = jnp.broadcast_to(total[None], sum_ref.shape)
    for copy in copies[1:]:
        copy.wait()


def momentum_kernel(core_ref, factor_ref, keep_ref, give_ref, out_ref):
    factor = factor_ref[:1, :1]
    keep, give = halves(core_ref, out_ref.shape[1])
    for i in range(out_ref.shape[0]):
        out_ref[i, keep, :] = 0.95 * keep_ref[1, i] + keep_ref[0, i] * factor
        out_ref[i, give, :] = 0.95 * give_ref[1, i] + give_ref[0, i] * factor


def place_kernel(of_core, core_ref, values_ref, *refs):
    out_ref, sem = refs[-2:]
    groups, slice_rows, _ = out_ref.shape
    half = slice_rows // 2
    core = core_ref[0] if of_core else 1 - core_ref[0]
    source = values_ref.at[pl.ds(core * groups, groups)] if of_core else values_ref
    rows = pl.ds(pl.multiple_of(core * half, half), half)
    copy = pltpu.make_async_copy(source, out_ref.at[:, rows, :], sem)
    copy.start()
    copy.wait()


def place(of_core, core, values, shape, before=()):
    return pl.pallas_call(
        lambda *refs: place_kernel(of_core, *refs),
        out_shape=jax.ShapeDtypeStruct(shape, F32),
        in_specs=[SMEM, HBM] + [HBM] * len(before),
        out_specs=HBM,
        scratch_shapes=[pltpu.SemaphoreType.DMA],
        input_output_aliases={2: 0} if before else {},
        compiler_params=params(1),
        name="place",
    )(core, values, *before)


def mix_kernel(count, core_ref, sums_ref, keep_ref, got_ref, out_ref, factor_ref):
    groups = keep_ref.shape[1]
    total = jnp.sum(sums_ref[:, 0, :], axis=0, keepdims=True)[:, :1]
    factor = jnp.minimum(1.0, 0.5 / jnp.sqrt(total / count + 1e-06))
    factor_ref[...] = jnp.broadcast_to(factor, factor_ref.shape)
    mine = core_ref[0] * groups
    theirs = (1 - core_ref[0]) * groups

    def mix(g, m):
        clipped = g * factor
        return clipped + 0.95 * (0.95 * m + clipped)

    for i in range(groups):
        out_ref[mine + i] = mix(keep_ref[0, i], keep_ref[1, i])
        out_ref[theirs + i] = mix(got_ref[0, i], got_ref[1, i])


def gram_kernel(x_ref, g_ref, xh, xl, th, tl):
    split_both_ways(x_ref, xh, xl, th, tl)
    for i, j in PAIRS:
        g_ref[blk(i), blk(j)] = square(th, tl, xh, xl, i, j)


def poly_kernel(xh, xl, part_ref, other_ref, out_ref, raw, yh, yl, th, tl, gh, gl, mh, ml, nh, nl):
    split_both_ways(other_ref, yh, yl, th, tl)
    shape = (BLOCK, BLOCK)
    eye = (lax.broadcasted_iota(jnp.int32, shape, 0) == lax.broadcasted_iota(jnp.int32, shape, 1)).astype(F32)
    trace = jnp.zeros((1, 1), F32)
    for i, j in PAIRS:
        v = part_ref[blk(i), blk(j)] + square(th, tl, yh, yl, i, j)
        raw[blk(i), blk(j)] = v
        if i == j:
            trace = trace + jnp.sum(jnp.sum(v * eye, axis=0, keepdims=True), axis=1, keepdims=True)
    inverse = 1.0 / (jnp.sqrt(trace) + 1e-07)
    for i, j in PAIRS:
        v = raw[blk(i), blk(j)] * inverse * inverse
        raw[blk(i), blk(j)] = v
        put_symmetric(gh, gl, i, j, v)

    def polynomial(h, l, oh, ol):
        for i, j in PAIRS:
            v = A1 * raw[blk(i), blk(j)] + A2 * square(h, l, h, l, i, j)
            if i == j:
                v = v + A0 * eye
            put_symmetric(oh, ol, i, j, v)

    polynomial(gh, gl, mh, ml)
    for i, j in PAIRS:
        put_symmetric(nh, nl, i, j, square(mh, ml, mh, ml, i, j))
    rows = range(out_ref.shape[0] // BLOCK)
    for i in rows:
        for j in range(NB):
            v = dot3(xh[blk(i), :], xl[blk(i), :], mh[:, blk(j)], ml[:, blk(j)]) * inverse
            yh[blk(i), blk(j)], yl[blk(i), blk(j)] = split(v)
    for i, j in PAIRS:
        v = dot3(gh[blk(i), :], gl[blk(i), :], nh[:, blk(j)], nl[:, blk(j)])
        raw[blk(i), blk(j)] = v
        put_symmetric(mh, ml, i, j, v)
    polynomial(mh, ml, nh, nl)
    scale = 0.2 * math.sqrt(max(R, C))
    for i in rows:
        for j in range(NB):
            out_ref[blk(i), blk(j)] = scale * dot3(yh[blk(i), :], yl[blk(i), :], nh[:, blk(j)], nl[:, blk(j)])


def orthogonalize(own, other):
    n = own.shape[0]
    wide, tall, square = ((n, C), (C, n), (C, C))
    part, xh, xl = pl.pallas_call(
        gram_kernel,
        out_shape=(
            jax.ShapeDtypeStruct(square, F32),
            jax.ShapeDtypeStruct(wide, BF16),
            jax.ShapeDtypeStruct(wide, BF16),
        ),
        in_specs=[VMEM],
        out_specs=(VMEM,) * 3,
        scratch_shapes=[pltpu.VMEM(tall, BF16)] * 2,
        compiler_params=params(12),
        name="gram",
    )(own)
    return pl.pallas_call(
        poly_kernel,
        out_shape=jax.ShapeDtypeStruct(wide, F32),
        in_specs=[VMEM] * 4,
        out_specs=VMEM,
        scratch_shapes=[pltpu.VMEM(square, F32)]
        + [pltpu.VMEM(wide, BF16)] * 2
        + [pltpu.VMEM(tall, BF16)] * 2
        + [pltpu.VMEM(square, BF16)] * 6,
        compiler_params=params(24),
        name="poly",
    )(xh, xl, part, other)


def body(grad, momentum):
    groups, slice_rows, columns = grad.shape
    n_rows = lax.axis_size("dp")
    devices = n_rows * lax.axis_size("expert")
    core = lax.axis_index("expert") % 2
    half = slice_rows // 2
    count = groups * slice_rows * columns * devices

    core_index = core.reshape(1)
    pair = jax.ShapeDtypeStruct((2, groups, half, columns), F32)
    tile, keep, give = pl.pallas_call(
        prepare_kernel,
        out_shape=(jax.ShapeDtypeStruct((devices, 1, 128), F32), pair, pair),
        in_specs=[SMEM] + [PINNED] * 2,
        out_specs=(VMEM,) * 3,
        scratch_shapes=[pltpu.VMEM(grad.shape, grad.dtype), pltpu.SemaphoreType.DMA((3,))],
        compiler_params=params(8),
        name="prepare",
    )(
        core_index,
        pltpu.with_memory_space_constraint(grad, pltpu.HBM),
        pltpu.with_memory_space_constraint(momentum, pltpu.HBM),
    )
    sums = lax.all_to_all(tile, ("dp", "expert"), split_axis=0, concat_axis=0, tiled=True)
    got = swap_cores(give)
    outgoing, factor = pl.pallas_call(
        lambda *refs: mix_kernel(count, *refs),
        out_shape=(
            jax.ShapeDtypeStruct((n_rows, half, columns), F32),
            jax.ShapeDtypeStruct((8, 128), F32),
        ),
        in_specs=[SMEM] + [VMEM] * 3,
        out_specs=(VMEM, VMEM),
        compiler_params=params(10),
        name="mix",
    )(core_index, sums, keep, got)

    own = lax.all_to_all(outgoing, "dp", split_axis=0, concat_axis=0, tiled=True)
    factor, keep, give, own = lax.optimization_barrier((factor, keep, give, own))
    new_momentum = pl.pallas_call(
        momentum_kernel,
        out_shape=jax.ShapeDtypeStruct(momentum.shape, F32),
        in_specs=[SMEM] + [VMEM] * 3,
        out_specs=VMEM,
        compiler_params=params(8),
        name="momentum",
    )(core_index, factor, keep, give)
    own = own.reshape(n_rows * half, columns)
    finished = orthogonalize(own, swap_cores(own))

    finished, new_momentum = lax.optimization_barrier((finished, new_momentum))
    back = lax.all_to_all(
        finished.reshape(n_rows, half, columns), "dp", split_axis=0, concat_axis=0, tiled=True
    )
    theirs = lax.dynamic_slice_in_dim(back, (1 - core) * groups, groups, 0)
    got = swap_cores(theirs)
    update = place(True, core_index, back, grad.shape)
    update = place(False, core_index, got, grad.shape, (update,))
    return (new_momentum, update)


def solution(mesh):
    in_specs = (P("expert", "dp", None), P("expert", "dp", None))
    out_specs = (P("expert", "dp", None), P("expert", "dp", None))
    return jax.shard_map(body, mesh=mesh, in_specs=in_specs, out_specs=out_specs, check_vma=False)
```

```python
import math

import jax
import jax.numpy as jnp
from jax import lax
from jax.experimental import pallas as pl
from jax.experimental.pallas import tpu as pltpu
from jax.sharding import PartitionSpec as P

R = 1024
C = 768
ITERS = 2
BLOCK = 256
NB = C // BLOCK
PAIRS = [(i, j) for i in range(NB) for j in range(i, NB)]

A0, A1, A2 = 3.4445, -4.775, 2.0315
F32 = jnp.float32
BF16 = jnp.bfloat16

VMEM = pl.BlockSpec(memory_space=pltpu.VMEM)
SMEM = pl.BlockSpec(memory_space=pltpu.SMEM)
HBM = pl.BlockSpec(memory_space=pl.ANY)
PINNED = pl.BlockSpec(memory_space=pltpu.HBM)


def params(mib):
    return pltpu.CompilerParams(vmem_limit_bytes=mib << 20)


def swap_cores(x):
    n = lax.axis_size("expert")
    return lax.ppermute(x, "expert", [(i, i ^ 1) for i in range(n)])


def split(v):
    hi = v.astype(BF16)
    return hi, (v - hi.astype(F32)).astype(BF16)


def dot(a, b):
    return jnp.dot(a, b, preferred_element_type=F32)


def dot3(ah, al, bh, bl):
    return dot(ah, bh) + (dot(ah, bl) + dot(al, bh))


def blk(i):
    return pl.ds(i * BLOCK, BLOCK)


def square(rh, rl, ch, cl, i, j):
    if i != j:
        return dot3(rh[blk(i), :], rl[blk(i), :], ch[:, blk(j)], cl[:, blk(j)])
    cross = dot(rh[blk(i), :], cl[:, blk(j)])
    return dot(rh[blk(i), :], ch[:, blk(j)]) + (cross + cross.T)


def put_symmetric(h, l, i, j, v):
    h[blk(i), blk(j)], l[blk(i), blk(j)] = split(v)
    if i != j:
        h[blk(j), blk(i)], l[blk(j), blk(i)] = split(v.T)


def split_both_ways(x_ref, xh, xl, th, tl):
    for j in range(NB):
        v = x_ref[:, blk(j)]
        xh[:, blk(j)], xl[:, blk(j)] = split(v)
        th[blk(j), :], tl[blk(j), :] = split(v.T)


def halves(core_ref, slice_rows):
    half = slice_rows // 2
    core = core_ref[0]
    return (
        pl.ds(pl.multiple_of(core * half, half), half),
        pl.ds(pl.multiple_of((1 - core) * half, half), half),
    )


def prepare_kernel(core_ref, grad_ref, momentum_ref, sum_ref, keep_ref, give_ref, wide, sems):
    keep, give = halves(core_ref, grad_ref.shape[1])
    copies = [
        pltpu.make_async_copy(grad_ref, wide, sems.at[0]),
        pltpu.make_async_copy(momentum_ref.at[:, give, :], give_ref.at[1], sems.at[1]),
        pltpu.make_async_copy(momentum_ref.at[:, keep, :], keep_ref.at[1], sems.at[2]),
    ]
    for copy in copies:
        copy.start()
    copies[0].wait()
    total = jnp.zeros(give_ref.shape[2:], F32)
    for i in range(wide.shape[0]):
        kept = wide[i, keep, :].astype(F32)
        given = wide[i, give, :].astype(F32)
        total = total + kept * kept + given * given
        keep_ref[0, i] = kept
        give_ref[0, i] = given
    total = jnp.sum(jnp.sum(total, axis=0, keepdims=True), axis=1, keepdims=True)
    sum_ref[...] = jnp.broadcast_to(total[None], sum_ref.shape)
    for copy in copies[1:]:
        copy.wait()


def momentum_kernel(factor_ref, grad_ref, momentum_ref, out_ref, wide, held, sems):
    copies = [
        pltpu.make_async_copy(grad_ref, wide, sems.at[0]),
        pltpu.make_async_copy(momentum_ref, held, sems.at[1]),
    ]
    for copy in copies:
        copy.start()
    for copy in copies:
        copy.wait()
    factor = factor_ref[:1, :1]
    for i in range(out_ref.shape[0]):
        out_ref[i] = 0.95 * held[i] + wide[i].astype(F32) * factor


def copy_and_wait(source, target, sem):
    copy = pltpu.make_async_copy(source, target, sem)
    copy.start()
    copy.wait()


def place_own(core, values, shape):
    def kernel(core_ref, values_ref, out_ref, sem):
        keep, _ = halves(core_ref, shape[1])
        mine = pl.ds(core_ref[0] * shape[0], shape[0])
        copy_and_wait(values_ref.at[mine], out_ref.at[:, keep, :], sem)

    return pl.pallas_call(
        kernel,
        out_shape=jax.ShapeDtypeStruct(shape, F32),
        in_specs=[SMEM, HBM],
        out_specs=HBM,
        scratch_shapes=[pltpu.SemaphoreType.DMA],
        compiler_params=params(1),
        name="place_own",
    )(core, values)


def place_got(core, values, before):
    def kernel(core_ref, values_ref, before_ref, out_ref, sem):
        _, give = halves(core_ref, before.shape[1])
        copy_and_wait(values_ref, out_ref.at[:, give, :], sem)

    return pl.pallas_call(
        kernel,
        out_shape=jax.ShapeDtypeStruct(before.shape, F32),
        in_specs=[SMEM, HBM, HBM],
        out_specs=HBM,
        scratch_shapes=[pltpu.SemaphoreType.DMA],
        input_output_aliases={2: 0},
        compiler_params=params(1),
        name="place_got",
    )(core, values, before)


def mix_kernel(count, core_ref, sums_ref, keep_ref, got_ref, out_ref, factor_ref):
    groups = keep_ref.shape[1]
    total = jnp.sum(sums_ref[:, 0, :], axis=0, keepdims=True)[:, :1]
    factor = jnp.minimum(1.0, 0.5 / jnp.sqrt(total / count + 1e-06))
    factor_ref[...] = jnp.broadcast_to(factor, factor_ref.shape)
    mine = core_ref[0] * groups
    theirs = (1 - core_ref[0]) * groups

    def mix(g, m):
        clipped = g * factor
        return clipped + 0.95 * (0.95 * m + clipped)

    for i in range(groups):
        out_ref[mine + i] = mix(keep_ref[0, i], keep_ref[1, i])
        out_ref[theirs + i] = mix(got_ref[0, i], got_ref[1, i])


def gram_kernel(x_ref, g_ref, xh, xl, th, tl):
    split_both_ways(x_ref, xh, xl, th, tl)
    for i, j in PAIRS:
        g_ref[blk(i), blk(j)] = square(th, tl, xh, xl, i, j)


def more_gram_kernel(x_ref, before_ref, g_ref, xh, xl, th, tl):
    split_both_ways(x_ref, xh, xl, th, tl)
    for i, j in PAIRS:
        g_ref[blk(i), blk(j)] = before_ref[blk(i), blk(j)] + square(th, tl, xh, xl, i, j)


def poly_kernel(xh, xl, part_ref, other_ref, out_ref, raw, yh, yl, th, tl, gh, gl, mh, ml, nh, nl):
    some = pl.ds(0, other_ref.shape[0])
    oh, ol = yh.at[some], yl.at[some]
    split_both_ways(other_ref, oh, ol, th, tl)
    shape = (BLOCK, BLOCK)
    eye = (lax.broadcasted_iota(jnp.int32, shape, 0) == lax.broadcasted_iota(jnp.int32, shape, 1)).astype(F32)
    trace = jnp.zeros((1, 1), F32)
    for i, j in PAIRS:
        v = part_ref[blk(i), blk(j)] + square(th, tl, oh, ol, i, j)
        raw[blk(i), blk(j)] = v
        put_symmetric(gh, gl, i, j, v)
        if i == j:
            trace = trace + jnp.sum(jnp.sum(v * eye, axis=0, keepdims=True), axis=1, keepdims=True)
    inverse = 1.0 / (jnp.sqrt(trace) + 1e-07)
    inverse2 = inverse * inverse

    def polynomial(h, l, ph, pl_, linear, quadratic):
        for i, j in PAIRS:
            v = linear * raw[blk(i), blk(j)] + quadratic * square(h, l, h, l, i, j)
            if i == j:
                v = v + A0 * eye
            put_symmetric(ph, pl_, i, j, v)

    polynomial(gh, gl, mh, ml, A1 * inverse2, A2 * inverse2 * inverse2)
    for i, j in PAIRS:
        put_symmetric(nh, nl, i, j, square(mh, ml, mh, ml, i, j))
    rows = range(out_ref.shape[0] // BLOCK)
    for i in rows:
        for j in range(NB):
            v = dot3(xh[blk(i), :], xl[blk(i), :], mh[:, blk(j)], ml[:, blk(j)]) * inverse
            yh[blk(i), blk(j)], yl[blk(i), blk(j)] = split(v)
    for i, j in PAIRS:
        v = inverse2 * dot3(gh[blk(i), :], gl[blk(i), :], nh[:, blk(j)], nl[:, blk(j)])
        raw[blk(i), blk(j)] = v
        put_symmetric(mh, ml, i, j, v)
    polynomial(mh, ml, nh, nl, A1, A2)
    scale = 0.2 * math.sqrt(max(R, C))
    for i in rows:
        for j in range(NB):
            out_ref[blk(i), blk(j)] = scale * dot3(yh[blk(i), :], yl[blk(i), :], nh[:, blk(j)], nl[:, blk(j)])


def orthogonalize(own):
    n = own.shape[0]
    first, last = swap_cores(own[: n // 2]), swap_cores(own[n // 2 :])
    wide, square_ = ((n, C), (C, C))
    part, xh, xl = pl.pallas_call(
        gram_kernel,
        out_shape=(
            jax.ShapeDtypeStruct(square_, F32),
            jax.ShapeDtypeStruct(wide, BF16),
            jax.ShapeDtypeStruct(wide, BF16),
        ),
        in_specs=[VMEM],
        out_specs=(VMEM,) * 3,
        scratch_shapes=[pltpu.VMEM((C, n), BF16)] * 2,
        compiler_params=params(12),
        name="gram",
    )(own)
    split_scratch = [pltpu.VMEM((n // 2, C), BF16)] * 2 + [pltpu.VMEM((C, n // 2), BF16)] * 2
    part = pl.pallas_call(
        more_gram_kernel,
        out_shape=jax.ShapeDtypeStruct(square_, F32),
        in_specs=[VMEM] * 2,
        out_specs=VMEM,
        scratch_shapes=split_scratch,
        compiler_params=params(12),
        name="more_gram",
    )(first, part)
    return pl.pallas_call(
        poly_kernel,
        out_shape=jax.ShapeDtypeStruct(wide, F32),
        in_specs=[VMEM] * 4,
        out_specs=VMEM,
        scratch_shapes=[pltpu.VMEM(square_, F32)]
        + [pltpu.VMEM(wide, BF16)] * 2
        + split_scratch[2:]
        + [pltpu.VMEM(square_, BF16)] * 6,
        compiler_params=params(24),
        name="poly",
    )(xh, xl, part, last)


def body(grad, momentum):
    groups, slice_rows, columns = grad.shape
    n_rows = lax.axis_size("dp")
    devices = n_rows * lax.axis_size("expert")
    core = lax.axis_index("expert") % 2
    half = slice_rows // 2
    count = groups * slice_rows * columns * devices

    core_index = core.reshape(1)
    inputs = [pltpu.with_memory_space_constraint(x, pltpu.HBM) for x in (grad, momentum)]
    pair = jax.ShapeDtypeStruct((2, groups, half, columns), F32)
    tile, keep, give = pl.pallas_call(
        prepare_kernel,
        out_shape=(jax.ShapeDtypeStruct((devices, 1, 128), F32), pair, pair),
        in_specs=[SMEM] + [PINNED] * 2,
        out_specs=(VMEM,) * 3,
        scratch_shapes=[pltpu.VMEM(grad.shape, grad.dtype), pltpu.SemaphoreType.DMA((3,))],
        compiler_params=params(8),
        name="prepare",
    )(core_index, *inputs)
    sums = lax.all_to_all(tile, ("dp", "expert"), split_axis=0, concat_axis=0, tiled=True)
    got = swap_cores(give)
    outgoing, factor = pl.pallas_call(
        lambda *refs: mix_kernel(count, *refs),
        out_shape=(
            jax.ShapeDtypeStruct((n_rows, half, columns), F32),
            jax.ShapeDtypeStruct((8, 128), F32),
        ),
        in_specs=[SMEM] + [VMEM] * 3,
        out_specs=(VMEM, VMEM),
        compiler_params=params(10),
        name="mix",
    )(core_index, sums, keep, got)

    own = lax.all_to_all(outgoing, "dp", split_axis=0, concat_axis=0, tiled=True)
    finished = orthogonalize(own.reshape(n_rows * half, columns))

    finished, factor = lax.optimization_barrier((finished, factor))
    back = lax.all_to_all(
        finished.reshape(n_rows, half, columns), "dp", split_axis=0, concat_axis=0, tiled=True
    )
    new_momentum = pl.pallas_call(
        momentum_kernel,
        out_shape=jax.ShapeDtypeStruct(momentum.shape, F32),
        in_specs=[VMEM] + [PINNED] * 2,
        out_specs=VMEM,
        scratch_shapes=[
            pltpu.VMEM(grad.shape, grad.dtype),
            pltpu.VMEM(momentum.shape, F32),
            pltpu.SemaphoreType.DMA((2,)),
        ],
        compiler_params=params(10),
        name="momentum",
    )(factor, *inputs)
    back, new_momentum = lax.optimization_barrier((back, new_momentum))

    theirs = lax.dynamic_slice(
        back, ((1 - core) * groups, 0, 0), (groups, half, columns), allow_negative_indices=False
    )
    got = swap_cores(theirs)
    update = place_own(core_index, back, grad.shape)
    update = place_got(core_index, got, update)
    return (new_momentum, update)


def solution(mesh):
    in_specs = (P("expert", "dp", None), P("expert", "dp", None))
    out_specs = (P("expert", "dp", None), P("expert", "dp", None))
    return jax.shard_map(body, mesh=mesh, in_specs=in_specs, out_specs=out_specs, check_vma=False)
```

```python
import math

import jax
import jax.numpy as jnp
from jax import lax
from jax.experimental import pallas as pl
from jax.experimental.pallas import tpu as pltpu
from jax.sharding import PartitionSpec as P

R = 1024
C = 768
ITERS = 2
BLOCK = 256
NB = C // BLOCK
Y = 4
PAIRS = [(i, j) for i in range(NB) for j in range(i, NB)]

A0, A1, A2 = 3.4445, -4.775, 2.0315
F32 = jnp.float32
BF16 = jnp.bfloat16

VMEM = pl.BlockSpec(memory_space=pltpu.VMEM)
SMEM = pl.BlockSpec(memory_space=pltpu.SMEM)
HBM = pl.BlockSpec(memory_space=pl.ANY)
PINNED = pl.BlockSpec(memory_space=pltpu.HBM)


def params(mib):
    return pltpu.CompilerParams(vmem_limit_bytes=mib << 20)


def swap_cores(x):
    n = lax.axis_size("expert")
    return lax.ppermute(x, "expert", [(i, i ^ 1) for i in range(n)])


def exchange_rows(x):
    z_size = lax.axis_size("dp") // Y
    fold = [z for k in range(z_size // 2) for z in (k, z_size - 1 - k)]
    group = [z * Y + y for y in range(Y) for z in fold]
    return lax.all_to_all(
        x, "dp", split_axis=0, concat_axis=0, tiled=True, axis_index_groups=[group]
    )


def split(v):
    hi = v.astype(BF16)
    return hi, (v - hi.astype(F32)).astype(BF16)


def dot(a, b):
    return jnp.dot(a, b, preferred_element_type=F32)


def dot3(ah, al, bh, bl):
    return dot(ah, bh) + (dot(ah, bl) + dot(al, bh))


def blk(i):
    return pl.ds(i * BLOCK, BLOCK)


def square(rh, rl, ch, cl, i, j):
    if i != j:
        return dot3(rh[blk(i), :], rl[blk(i), :], ch[:, blk(j)], cl[:, blk(j)])
    cross = dot(rh[blk(i), :], cl[:, blk(j)])
    return dot(rh[blk(i), :], ch[:, blk(j)]) + (cross + cross.T)


def put_symmetric(h, l, i, j, v):
    h[blk(i), blk(j)], l[blk(i), blk(j)] = split(v)
    if i != j:
        h[blk(j), blk(i)], l[blk(j), blk(i)] = split(v.T)


def split_both_ways(x_ref, xh, xl, th, tl):
    for j in range(NB):
        v = x_ref[:, blk(j)]
        xh[:, blk(j)], xl[:, blk(j)] = split(v)
        th[blk(j), :], tl[blk(j), :] = split(v.T)


def halves(core_ref, slice_rows):
    half = slice_rows // 2
    core = core_ref[0]
    return (
        pl.ds(pl.multiple_of(core * half, half), half),
        pl.ds(pl.multiple_of((1 - core) * half, half), half),
    )


def prepare_kernel(core_ref, grad_ref, momentum_ref, sum_ref, keep_ref, give_ref, wide, sems):
    keep, give = halves(core_ref, grad_ref.shape[1])
    copies = [
        pltpu.make_async_copy(grad_ref, wide, sems.at[0]),
        pltpu.make_async_copy(momentum_ref.at[:, give, :], give_ref.at[1], sems.at[1]),
        pltpu.make_async_copy(momentum_ref.at[:, keep, :], keep_ref.at[1], sems.at[2]),
    ]
    for copy in copies:
        copy.start()
    copies[0].wait()
    total = jnp.zeros(give_ref.shape[2:], F32)
    for i in range(wide.shape[0]):
        kept = wide[i, keep, :].astype(F32)
        given = wide[i, give, :].astype(F32)
        total = total + kept * kept + given * given
        keep_ref[0, i] = kept
        give_ref[0, i] = given
    total = jnp.sum(jnp.sum(total, axis=0, keepdims=True), axis=1, keepdims=True)
    sum_ref[...] = jnp.broadcast_to(total[None], sum_ref.shape)
    for copy in copies[1:]:
        copy.wait()


def momentum_kernel(factor_ref, grad_ref, momentum_ref, out_ref, wide, held, sems):
    copies = [
        pltpu.make_async_copy(grad_ref, wide, sems.at[0]),
        pltpu.make_async_copy(momentum_ref, held, sems.at[1]),
    ]
    for copy in copies:
        copy.start()
    for copy in copies:
        copy.wait()
    factor = factor_ref[:1, :1]
    for i in range(out_ref.shape[0]):
        out_ref[i] = 0.95 * held[i] + wide[i].astype(F32) * factor


def copy_and_wait(source, target, sem):
    copy = pltpu.make_async_copy(source, target, sem)
    copy.start()
    copy.wait()


def place_own(core, values, shape):
    def kernel(core_ref, values_ref, out_ref, sem):
        keep, _ = halves(core_ref, shape[1])
        mine = pl.ds(core_ref[0] * shape[0], shape[0])
        copy_and_wait(values_ref.at[mine], out_ref.at[:, keep, :], sem)

    return pl.pallas_call(
        kernel,
        out_shape=jax.ShapeDtypeStruct(shape, F32),
        in_specs=[SMEM, HBM],
        out_specs=HBM,
        scratch_shapes=[pltpu.SemaphoreType.DMA],
        compiler_params=params(1),
        name="place_own",
    )(core, values)


def place_got(core, values, before):
    def kernel(core_ref, values_ref, before_ref, out_ref, sem):
        _, give = halves(core_ref, before.shape[1])
        copy_and_wait(values_ref, out_ref.at[:, give, :], sem)

    return pl.pallas_call(
        kernel,
        out_shape=jax.ShapeDtypeStruct(before.shape, F32),
        in_specs=[SMEM, HBM, HBM],
        out_specs=HBM,
        scratch_shapes=[pltpu.SemaphoreType.DMA],
        input_output_aliases={2: 0},
        compiler_params=params(1),
        name="place_got",
    )(core, values, before)


def mix_kernel(count, core_ref, sums_ref, keep_ref, got_ref, out_ref, factor_ref):
    groups = keep_ref.shape[1]
    total = jnp.sum(sums_ref[:, 0, :], axis=0, keepdims=True)[:, :1]
    factor = jnp.minimum(1.0, 0.5 / jnp.sqrt(total / count + 1e-06))
    factor_ref[...] = jnp.broadcast_to(factor, factor_ref.shape)
    mine = core_ref[0] * groups
    theirs = (1 - core_ref[0]) * groups

    def mix(g, m):
        clipped = g * factor
        return clipped + 0.95 * (0.95 * m + clipped)

    for i in range(groups):
        out_ref[mine + i] = mix(keep_ref[0, i], keep_ref[1, i])
        out_ref[theirs + i] = mix(got_ref[0, i], got_ref[1, i])


def gram_kernel(x_ref, g_ref, xh, xl, th, tl):
    split_both_ways(x_ref, xh, xl, th, tl)
    for i, j in PAIRS:
        g_ref[blk(i), blk(j)] = square(th, tl, xh, xl, i, j)


def more_gram_kernel(x_ref, before_ref, g_ref, xh, xl, th, tl):
    split_both_ways(x_ref, xh, xl, th, tl)
    for i, j in PAIRS:
        g_ref[blk(i), blk(j)] = before_ref[blk(i), blk(j)] + square(th, tl, xh, xl, i, j)


def poly_kernel(
    xh, xl, part_ref, other_ref, out_ref, raw, yh, yl, th, tl, gh, gl, mh, ml, nh, nl, stage, sems
):
    some = pl.ds(0, other_ref.shape[0])
    oh, ol = yh.at[some], yl.at[some]
    split_both_ways(other_ref, oh, ol, th, tl)
    shape = (BLOCK, BLOCK)
    eye = (lax.broadcasted_iota(jnp.int32, shape, 0) == lax.broadcasted_iota(jnp.int32, shape, 1)).astype(F32)
    trace = jnp.zeros((1, 1), F32)
    for i, j in PAIRS:
        v = part_ref[blk(i), blk(j)] + square(th, tl, oh, ol, i, j)
        raw[blk(i), blk(j)] = v
        put_symmetric(gh, gl, i, j, v)
        if i == j:
            trace = trace + jnp.sum(jnp.sum(v * eye, axis=0, keepdims=True), axis=1, keepdims=True)
    inverse = 1.0 / (jnp.sqrt(trace) + 1e-07)
    inverse2 = inverse * inverse

    def polynomial(h, l, ph, pl_, linear, quadratic):
        for i, j in PAIRS:
            v = linear * raw[blk(i), blk(j)] + quadratic * square(h, l, h, l, i, j)
            if i == j:
                v = v + A0 * eye
            put_symmetric(ph, pl_, i, j, v)

    polynomial(gh, gl, mh, ml, A1 * inverse2, A2 * inverse2 * inverse2)
    for i, j in PAIRS:
        put_symmetric(nh, nl, i, j, square(mh, ml, mh, ml, i, j))
    rows = range(out_ref.shape[0] // BLOCK)
    for i in rows:
        for j in range(NB):
            v = dot3(xh[blk(i), :], xl[blk(i), :], mh[:, blk(j)], ml[:, blk(j)]) * inverse
            yh[blk(i), blk(j)], yl[blk(i), blk(j)] = split(v)
    for i, j in PAIRS:
        v = inverse2 * dot3(gh[blk(i), :], gl[blk(i), :], nh[:, blk(j)], nl[:, blk(j)])
        raw[blk(i), blk(j)] = v
        put_symmetric(mh, ml, i, j, v)
    polynomial(mh, ml, nh, nl, A1, A2)
    scale = 0.2 * math.sqrt(max(R, C))
    copies = []
    for i in rows:
        for j in range(NB):
            place = (blk(i), blk(j))
            stage[place] = scale * dot3(yh[blk(i), :], yl[blk(i), :], nh[:, blk(j)], nl[:, blk(j)])
            copies.append(pltpu.make_async_copy(stage.at[place], out_ref.at[place], sems.at[len(copies)]))
            copies[-1].start()
    for copy in copies:
        copy.wait()


def orthogonalize(own):
    n = own.shape[0]
    first, last = swap_cores(own[: n // 2]), swap_cores(own[n // 2 :])
    wide, square_ = ((n, C), (C, C))
    part, xh, xl = pl.pallas_call(
        gram_kernel,
        out_shape=(
            jax.ShapeDtypeStruct(square_, F32),
            jax.ShapeDtypeStruct(wide, BF16),
            jax.ShapeDtypeStruct(wide, BF16),
        ),
        in_specs=[VMEM],
        out_specs=(VMEM,) * 3,
        scratch_shapes=[pltpu.VMEM((C, n), BF16)] * 2,
        compiler_params=params(12),
        name="gram",
    )(own)
    split_scratch = [pltpu.VMEM((n // 2, C), BF16)] * 2 + [pltpu.VMEM((C, n // 2), BF16)] * 2
    part = pl.pallas_call(
        more_gram_kernel,
        out_shape=jax.ShapeDtypeStruct(square_, F32),
        in_specs=[VMEM] * 2,
        out_specs=VMEM,
        scratch_shapes=split_scratch,
        compiler_params=params(12),
        name="more_gram",
    )(first, part)
    return pl.pallas_call(
        poly_kernel,
        out_shape=jax.ShapeDtypeStruct(wide, F32),
        in_specs=[VMEM] * 4,
        out_specs=HBM,
        scratch_shapes=[pltpu.VMEM(square_, F32)]
        + [pltpu.VMEM(wide, BF16)] * 2
        + split_scratch[2:]
        + [pltpu.VMEM(square_, BF16)] * 6
        + [pltpu.VMEM(wide, F32), pltpu.SemaphoreType.DMA((n // BLOCK * NB,))],
        compiler_params=params(24),
        name="poly",
    )(xh, xl, part, last)


def body(grad, momentum):
    groups, slice_rows, columns = grad.shape
    n_rows = lax.axis_size("dp")
    devices = n_rows * lax.axis_size("expert")
    core = lax.axis_index("expert") % 2
    half = slice_rows // 2
    count = groups * slice_rows * columns * devices

    core_index = core.reshape(1)
    inputs = [pltpu.with_memory_space_constraint(x, pltpu.HBM) for x in (grad, momentum)]
    pair = jax.ShapeDtypeStruct((2, groups, half, columns), F32)
    tile, keep, give = pl.pallas_call(
        prepare_kernel,
        out_shape=(jax.ShapeDtypeStruct((devices, 1, 128), F32), pair, pair),
        in_specs=[SMEM] + [PINNED] * 2,
        out_specs=(VMEM,) * 3,
        scratch_shapes=[pltpu.VMEM(grad.shape, grad.dtype), pltpu.SemaphoreType.DMA((3,))],
        compiler_params=params(8),
        name="prepare",
    )(core_index, *inputs)
    sums = lax.all_to_all(tile, ("dp", "expert"), split_axis=0, concat_axis=0, tiled=True)
    got = swap_cores(give)
    outgoing, factor = pl.pallas_call(
        lambda *refs: mix_kernel(count, *refs),
        out_shape=(
            jax.ShapeDtypeStruct((n_rows, half, columns), F32),
            jax.ShapeDtypeStruct((8, 128), F32),
        ),
        in_specs=[SMEM] + [VMEM] * 3,
        out_specs=(VMEM, VMEM),
        compiler_params=params(10),
        name="mix",
    )(core_index, sums, keep, got)

    own = exchange_rows(outgoing)
    finished = orthogonalize(own.reshape(n_rows * half, columns))

    finished, factor = lax.optimization_barrier((finished, factor))
    back = exchange_rows(finished.reshape(n_rows, half, columns))
    new_momentum = pl.pallas_call(
        momentum_kernel,
        out_shape=jax.ShapeDtypeStruct(momentum.shape, F32),
        in_specs=[VMEM] + [PINNED] * 2,
        out_specs=VMEM,
        scratch_shapes=[
            pltpu.VMEM(grad.shape, grad.dtype),
            pltpu.VMEM(momentum.shape, F32),
            pltpu.SemaphoreType.DMA((2,)),
        ],
        compiler_params=params(10),
        name="momentum",
    )(factor, *inputs)
    back, new_momentum = lax.optimization_barrier((back, new_momentum))

    theirs = lax.dynamic_slice(
        back, ((1 - core) * groups, 0, 0), (groups, half, columns), allow_negative_indices=False
    )
    got = swap_cores(theirs)
    update = place_own(core_index, back, grad.shape)
    update = place_got(core_index, got, update)
    return (new_momentum, update)


def solution(mesh):
    in_specs = (P("expert", "dp", None), P("expert", "dp", None))
    out_specs = (P("expert", "dp", None), P("expert", "dp", None))
    return jax.shard_map(body, mesh=mesh, in_specs=in_specs, out_specs=out_specs, check_vma=False)
```
